256 devices in a mesh: dp: 32 (over x, y, core), tensor: 8 (over z).
Axes of the slice: x: 4, y: 4, z: 8, core: 2. Of those that a mesh axis runs over, the one named last changes fastest.
Arguments:
- layer_input: bfloat16 [65536, 4096], P('dp', 'tensor'), may hold values from -54 to 54
- queries: bfloat16 [65536, 2048], P('dp', 'tensor'), may hold values from -6 to 6
- keys_values: bfloat16 [65536, 2, 1024], P('dp', None, 'tensor'), may hold values from -6 to 6
- out_grads: bfloat16 [65536, 2048], P('dp', 'tensor'), may hold values from -6 to 6
- log_sums: bfloat16 [65536, 16], P('dp', 'tensor'), may hold values from 2.5 to 5.5
- deltas: bfloat16 [65536, 16], P('dp', 'tensor'), may hold values from -1.5 to 1.5
- tile_fill: int32 [32, 16], replicated, may hold values from 1 to 128, as said below
- tile_cont: int32 [32, 16], replicated, may hold values from 0 to 1, as said below
- moment_first: float32 [4096, 2, 1024], P(('tensor', 'dp')), may hold values from -2 to 2
- moment_second: float32 [2, 8], replicated, may hold values from 0.05 to 0.5
Outputs:
- update: float32 [4096, 2, 1024], P(('tensor', 'dp'))
- new_first: float32 [4096, 2, 1024], P(('tensor', 'dp'))
- new_second: float32 [2, 8], replicated
The draws below stay inside these ranges and needn't reach their ends.
Inputs may be any that keep to these rules, and one draw needn't show every extreme that they name: `tile_fill`: a tile followed by a tile with tile_cont 1 has all 128 positions live. Documents span one or two tiles: tile_cont is 0 for the first tile of each group and never 1 for two tiles in a row.
All inputs are finite; a program needn't handle non-finite values.
Results may differ from the reference program's by a relative error of at most 0.0055.
Values may be sent and summed in bfloat16 or wider, within the bound.
No kernel may reach another device: no remote copies, remote signals or barrier semaphores. Data moves between devices by JAX's collectives and lax.ppermute only.
A program may use at most 64 MiB of HBM per device.

```python
import math
import jax
import jax.numpy as jnp
from jax import lax

D = 4096
HQ = 16
HK = 8
HD = 128
BLK = 128
TILES_DEV = 16
TOKENS = 65536
N_DP = 32


def tile_layout(key):
    key = jax.random.fold_in(key, 7)
    key_bits, key_fill = jax.random.split(key)
    coin_bits = jax.random.randint(key_bits, (N_DP, TILES_DEV), 0, 2)
    tile_index = jnp.arange(TILES_DEV)

    def advance(previous, column):
        col_bits, position = column
        linked = jnp.where(position == 1, 1, jnp.where(position == 0, 0, col_bits * (1 - previous)))
        linked = linked.astype(jnp.int32)
        return (linked, linked)
    final_state, linked = lax.scan(advance, jnp.zeros((N_DP,), jnp.int32), (coin_bits.T, tile_index))
    tile_cont = linked.T.astype(jnp.int32)
    following = jnp.concatenate([tile_cont[:, 1:], jnp.zeros_like(tile_cont[:, :1])], 1)
    raw_fill = jax.random.randint(key_fill, (N_DP, TILES_DEV), 1, BLK + 1)
    tile_fill = jnp.where(following == 1, BLK, raw_fill).astype(jnp.int32)
    return (tile_fill, tile_cont)


def draw_tile_fill(key, part):
    return tile_layout(key)[0]


def draw_tile_cont(key, part):
    return tile_layout(key)[1]


def draw_layer_input(key, part):
    key = jax.random.fold_in(key, 11)
    key_cols, key_vals = jax.random.split(key, 2)
    columns = jnp.arange(D, dtype=jnp.float32) / D
    spread = jnp.exp(jax.random.uniform(key_cols, (D,), jnp.float32, math.log(0.3), math.log(3.0)))
    col_ramp = 1.0 + 2.0 * columns
    base_vals = jnp.clip(jax.random.normal(key_vals, (TOKENS, D), jnp.float32), -6.0, 6.0)
    return (base_vals * spread[None, :] * col_ramp[None, :]).astype(jnp.bfloat16)


def steps_of(rng, extent, shards, smallest, largest):
    gain, own = 1.0, jax.random.fold_in(rng, 6)
    for dim, shards_of in shards:
        draws = jnp.exp(jax.random.uniform(jax.random.fold_in(own, dim), (shards_of,), jnp.float32, smallest / len(shards), largest / len(shards)))
        gain = gain * jnp.repeat(draws, extent[dim] // shards_of).reshape([-1 if axis == dim else 1 for axis in range(len(extent))])
    return gain


def scatter_about(own_key, shape, scale, reach, pieces=(), held_as=jnp.bfloat16):
    drawn = jax.random.normal(own_key, shape, jnp.float32) * scale
    if len(pieces) > 0:
        drawn = steps_of(own_key, shape, pieces, -0.22, 0.18) * drawn
    return jnp.clip(drawn, min=-reach, max=reach).astype(held_as)


def setup_inputs(seed: int = 0) -> dict:
    arg_keys = jax.random.split(jax.random.key(seed), 11)
    layer_input = draw_layer_input(jax.random.fold_in(arg_keys[10], 71), 0)
    queries = scatter_about(arg_keys[1], (TOKENS, HQ * HD), 1.0, 6.0, ((0, 32), (1, 8)))
    keys_values = scatter_about(arg_keys[2], (TOKENS, 2, HK * HD), 1.0, 6.0, ((0, 32), (2, 8)))
    out_grads = scatter_about(arg_keys[3], (TOKENS, HQ * HD), 1.0, 6.0, ((0, 32), (1, 8)))
    log_sums = jnp.clip(2.5 + 3.0 * jax.random.uniform(arg_keys[4], (TOKENS, HQ), jnp.float32) ** steps_of(arg_keys[4], (TOKENS, HQ), ((0, 32), (1, 8)), -0.2, 0.2), 2.5, 5.5).astype(jnp.bfloat16)
    deltas = scatter_about(arg_keys[5], (TOKENS, HQ), 0.3, 1.5, ((0, 32), (1, 8)))
    tile_fill = draw_tile_fill(jax.random.fold_in(arg_keys[10], 71), 0)
    tile_cont = draw_tile_cont(jax.random.fold_in(arg_keys[10], 71), 0)
    moment_first = scatter_about(arg_keys[8], (D, 2, HK * HD), 0.3, 2.0, ((0, 256),), jnp.float32)
    moment_second = jnp.clip(jnp.exp(jax.random.uniform(arg_keys[9], (2, HK), jnp.float32, math.log(0.05), math.log(0.5))), 0.05, 0.5)
    return {"layer_input": layer_input, "queries": queries, "keys_values": keys_values, "out_grads": out_grads, "log_sums": log_sums, "deltas": deltas, "tile_fill": tile_fill, "tile_cont": tile_cont, "moment_first": moment_first, "moment_second": moment_second}


HIGHEST_PRECISION = lax.Precision.HIGHEST

def band_grads(q_tiles, k_tiles, v_tiles, do_tiles, lse_tiles, delta_tiles, fill_tiles, cont_tiles):
    tile_total, block_len, groups, head_width = q_tiles.shape
    scale_qk = head_width ** (-0.5)
    q_full = q_tiles.astype(jnp.float32)
    do_full = do_tiles.astype(jnp.float32)
    k_full = k_tiles.astype(jnp.float32)
    v_full = v_tiles.astype(jnp.float32)
    zero_tile = jnp.zeros_like(k_full[:1])
    k_window = jnp.concatenate([jnp.concatenate([zero_tile, k_full[:-1]], 0), k_full], 1)
    v_window = jnp.concatenate([jnp.concatenate([zero_tile, v_full[:-1]], 0), v_full], 1)
    places = jnp.arange(block_len)
    live_rows = places[None, :] < fill_tiles[:, None]
    causal = places[:, None] >= places[None, :]
    own_part = live_rows[:, :, None] & causal[None]
    prev_part = live_rows[:, :, None] & (cont_tiles[:, None, None] == 1) & (places[None, None, :] >= 0)
    allowed = jnp.concatenate([prev_part, own_part], 2)[:, None]
    scores = jnp.einsum('sqgd,skd->sgqk', q_full, k_window, precision=HIGHEST_PRECISION) * scale_qk
    lse_rows = jnp.swapaxes(lse_tiles.astype(jnp.float32), 1, 2)[..., None]
    delta_rows = jnp.swapaxes(delta_tiles.astype(jnp.float32), 1, 2)[..., None]
    prob_vals = jnp.where(allowed, jnp.exp(scores - lse_rows), 0.0)
    dprobs = jnp.einsum('sqgd,skd->sgqk', do_full, v_window, precision=HIGHEST_PRECISION)
    dscores = prob_vals * (dprobs - delta_rows)
    prob_half = lax.optimization_barrier(prob_vals.astype(jnp.bfloat16)).astype(jnp.float32)
    score_half = lax.optimization_barrier(dscores.astype(jnp.bfloat16)).astype(jnp.float32)
    value_grad = jnp.einsum('sgqk,sqgd->skd', prob_half, do_full, precision=HIGHEST_PRECISION)
    key_grad = jnp.einsum('sgqk,sqgd->skd', score_half, q_full, precision=HIGHEST_PRECISION) * scale_qk
    key_out = key_grad[:, block_len:] + jnp.concatenate([key_grad[1:, :block_len], jnp.zeros_like(key_grad[:1, :block_len])], 0)
    value_out = value_grad[:, block_len:] + jnp.concatenate([value_grad[1:, :block_len], jnp.zeros_like(value_grad[:1, :block_len])], 0)
    return (key_out, value_out)

def reference(layer_input, queries, keys_values, out_grads, log_sums, deltas, tile_fill, tile_cont, moment_first, moment_second):
    tiles_all = N_DP * TILES_DEV
    groups = HQ // HK
    q_heads = queries.reshape(tiles_all, BLK, HK, groups, HD).transpose(2, 0, 1, 3, 4)
    do_heads = out_grads.reshape(tiles_all, BLK, HK, groups, HD).transpose(2, 0, 1, 3, 4)
    k_heads = keys_values[:, 0].reshape(tiles_all, BLK, HK, HD).transpose(2, 0, 1, 3)
    v_heads = keys_values[:, 1].reshape(tiles_all, BLK, HK, HD).transpose(2, 0, 1, 3)
    lse_heads = log_sums.reshape(tiles_all, BLK, HK, groups).transpose(2, 0, 1, 3)
    delta_heads = deltas.reshape(tiles_all, BLK, HK, groups).transpose(2, 0, 1, 3)
    fill_flat = tile_fill.reshape(-1)
    cont_flat = tile_cont.reshape(-1)

    def one_head(operands):
        q_one, k_one, v_one, do_one, lse_one, delta_one = operands
        key_out, value_out = band_grads(q_one, k_one, v_one, do_one, lse_one, delta_one, fill_flat, cont_flat)
        return jnp.stack([key_out, value_out], 2).astype(jnp.bfloat16)
    per_head = lax.map(one_head, (q_heads, k_heads, v_heads, do_heads, lse_heads, delta_heads))
    kv_grads = per_head.transpose(1, 2, 3, 0, 4).reshape(TOKENS, 2 * HK * HD)
    summed = lax.dot_general(layer_input, kv_grads, (((0,), (0,)), ((), ())), preferred_element_type=jnp.float32)
    proj_grads = summed.reshape(D, 2, HK * HD) / math.sqrt(TOKENS)
    new_first = 0.9 * moment_first + (1 - 0.9) * proj_grads
    squares = lax.optimization_barrier(jnp.sum(jnp.square(proj_grads).reshape(D, 2, HK, HD), axis=(0, 3)))
    new_second = 0.95 * moment_second + (1 - 0.95) * squares / (D * HD)
    step_size = jnp.sqrt(new_second / (1 - 0.95 ** 2)) + 1e-08
    update = ((new_first / (1 - 0.9 ** 2)).reshape(D, 2, HK, HD) / step_size[None, :, :, None]).reshape(D, 2, HK * HD)
    return (update, new_first, new_second)
```

```python
import functools
import math

import jax
import jax.numpy as jnp
from jax import lax
from jax.experimental import pallas as pl
from jax.experimental.pallas import tpu as pltpu
from jax.sharding import Mesh
from jax.sharding import PartitionSpec as P

D = 4096
HD = 128
BLK = 128
DP = ("dp_0", "dp_1", "dp_2")
TENSOR_DP = ("tensor", "dp_0", "dp_1", "dp_2")

ADAM_ONE = 0.9
ADAM_TWO = 0.95
ADAM_EPS = 1e-08

NT = (((1,), (1,)), ((), ()))
NN = (((1,), (0,)), ((), ()))
TN = (((0,), (0,)), ((), ()))


def attention_kernel(
    first,
    per_step,
    tile_count,
    fill_ref,
    cont_ref,
    q_ref,
    q_next_ref,
    do_ref,
    do_next_ref,
    kv_ref,
    lse_ref,
    lse_next_ref,
    delta_ref,
    delta_next_ref,
    out_ref,
):
    heads = q_ref.shape[1] // HD
    scale_qk = HD ** (-0.5)
    base = first + pl.program_id(0) * per_step
    for j in range(per_step):
        tile = base + j
        rows = pl.ds(j * BLK, BLK)
        after = jnp.minimum(tile + 1, tile_count - 1)
        fill_own = fill_ref[tile]
        linked = jnp.where(tile + 1 < tile_count, cont_ref[after], 0)
        fill_next = jnp.where(linked == 1, fill_ref[after], 0)

        def window(ref, next_ref, h):
            columns = slice(h * HD, (h + 1) * HD)
            own = ref[rows, columns]
            if j + 1 < per_step:
                follow = ref[pl.ds((j + 1) * BLK, BLK), columns]
            else:
                follow = next_ref[:, columns]
            return [own, follow]

        def stat(ref, next_ref, h):
            own = ref[h : h + 1, pl.ds(j * BLK, BLK)]
            if j + 1 < per_step:
                follow = ref[h : h + 1, pl.ds((j + 1) * BLK, BLK)]
            else:
                follow = next_ref[h : h + 1, :]
            return [own.astype(jnp.float32), follow.astype(jnp.float32)]

        def stack(pick, ref, next_ref, axis):
            return jnp.concatenate(sum([pick(ref, next_ref, h) for h in range(heads)], []), axis)

        q_all = stack(window, q_ref, q_next_ref, 0)
        do_all = stack(window, do_ref, do_next_ref, 0)
        lse_row = stack(stat, lse_ref, lse_next_ref, 1)
        delta_row = stack(stat, delta_ref, delta_next_ref, 1)
        keys = kv_ref[0, rows, :]
        values = kv_ref[1, rows, :]
        scores = lax.dot_general(keys, q_all, NT, preferred_element_type=jnp.float32) * scale_qk
        dprobs = lax.dot_general(values, do_all, NT, preferred_element_type=jnp.float32)
        key_place = lax.broadcasted_iota(jnp.int32, (BLK, BLK), 0)
        query_place = lax.broadcasted_iota(jnp.int32, (BLK, BLK), 1)
        own_part = (query_place < fill_own) & (query_place >= key_place)
        next_part = query_place < fill_next
        allowed = jnp.concatenate([own_part, next_part] * heads, 1)
        probs = jnp.where(allowed, jnp.exp(scores - lse_row), 0.0)
        dscores = probs * (dprobs - delta_row)
        value_grad = lax.dot_general(
            probs.astype(jnp.bfloat16), do_all, NN, preferred_element_type=jnp.float32
        )
        key_grad = (
            lax.dot_general(
                dscores.astype(jnp.bfloat16), q_all, NN, preferred_element_type=jnp.float32
            )
            * scale_qk
        )
        out_ref[rows, 0:HD] = key_grad.astype(jnp.bfloat16)
        out_ref[rows, HD : 2 * HD] = value_grad.astype(jnp.bfloat16)


def attention(first, count, per_step, fill, cont, queries, out_grads, keys_values, lse, delta):
    tile_count = queries.shape[0] // BLK
    width = queries.shape[1]
    steps = count // per_step
    offset = first // per_step

    def own(i, *_):
        return (offset + i, 0)

    def follow(i, *_):
        return (jnp.minimum(first + (i + 1) * per_step, tile_count - 1), 0)

    def own_lanes(i, *_):
        return (0, offset + i)

    def follow_lanes(i, *_):
        return (0, jnp.minimum(first + (i + 1) * per_step, tile_count - 1))

    rows = per_step * BLK
    heads = lse.shape[0]
    return pl.pallas_call(
        functools.partial(attention_kernel, first, per_step, tile_count),
        grid_spec=pltpu.PrefetchScalarGridSpec(
            num_scalar_prefetch=2,
            grid=(steps,),
            in_specs=[
                pl.BlockSpec((rows, width), own),
                pl.BlockSpec((BLK, width), follow),
                pl.BlockSpec((rows, width), own),
                pl.BlockSpec((BLK, width), follow),
                pl.BlockSpec((2, rows, HD), lambda i, *_: (0, offset + i, 0)),
                pl.BlockSpec((heads, rows), own_lanes),
                pl.BlockSpec((heads, BLK), follow_lanes),
                pl.BlockSpec((heads, rows), own_lanes),
                pl.BlockSpec((heads, BLK), follow_lanes),
            ],
            out_specs=pl.BlockSpec((rows, 2 * HD), lambda i, *_: (i, 0)),
        ),
        out_shape=jax.ShapeDtypeStruct((count * BLK, 2 * HD), jnp.bfloat16),
        compiler_params=pltpu.CompilerParams(vmem_limit_bytes=32 * 1024 * 1024),
        cost_estimate=pl.CostEstimate(
            flops=count * 8 * heads * BLK * 2 * BLK * HD,
            bytes_accessed=count * BLK * 10 * HD * 2,
            transcendentals=count * heads * 2 * BLK * BLK,
        ),
        name="attention_grads",
    )(fill, cont, queries, queries, out_grads, out_grads, keys_values, lse, lse, delta, delta)


def shifted(array, steps, length):
    return lax.ppermute(array, "tensor", [(i, (i + steps) % length) for i in range(length)])


def sum_at_owner(block, axes):
    length = lax.axis_size(axes)
    parts = block.reshape(length, -1, block.shape[1])
    arrived = lax.all_to_all(parts, axes, split_axis=0, concat_axis=0, tiled=True)
    return arrived.astype(jnp.float32).sum(axis=0)


def taken_together(array, axes):
    length = lax.axis_size(axes)
    everything = lax.all_to_all(
        jnp.broadcast_to(array[None], (length, *array.shape)), axes, 0, 0, tiled=True
    )
    return jnp.sum(everything, axis=0)


def per_device(
    layer_input,
    queries,
    keys_values,
    out_grads,
    log_sums,
    deltas,
    tile_fill,
    tile_cont,
    moment_first,
    moment_second,
):
    group_count = lax.axis_size(DP)
    ring = lax.axis_size("tensor")
    tile_count = tile_fill.shape[1]
    token_count = queries.shape[0]
    my_group = lax.axis_index(DP)
    place = lax.axis_index("tensor")
    fill = lax.dynamic_index_in_dim(tile_fill, my_group, 0, keepdims=False)
    cont = lax.dynamic_index_in_dim(tile_cont, my_group, 0, keepdims=False)
    kv = jnp.swapaxes(keys_values, 0, 1)
    half = tile_count // 2
    halves = [
        attention(first, half, 4, fill, cont, queries, out_grads, kv, log_sums.T, deltas.T)
        for first in (0, half)
    ]
    inputs = [layer_input[: half * BLK], layer_input[half * BLK :]]

    blocks = {0: list(halves)}
    right, left = list(halves), list(halves)
    far = ring // 2
    for step in range(1, far):
        for part in range(2):
            right[part] = shifted(right[part], 1, ring)
            left[part] = shifted(left[part], -1, ring)
        blocks[-step] = list(right)
        blocks[step] = list(left)
    blocks[far] = [shifted(right[0], 1, ring), shifted(left[1], -1, ring)]

    def product(offset):
        one, two = (
            lax.dot_general(x, b, TN, preferred_element_type=jnp.float32)
            for x, b in zip(inputs, blocks[offset])
        )
        return (one + two).astype(jnp.bfloat16)

    summed = {}
    for offsets in ((0, -1, 1), (-2, 2), (-3, 3, far)):
        together = jnp.concatenate([product(o) for o in offsets], 1)
        total = sum_at_owner(together, DP)
        for i, o in enumerate(offsets):
            summed[o % ring] = total[:, i * 2 * HD : (i + 1) * 2 * HD]

    rows = moment_first.shape[0]
    in_turn = jnp.stack([summed[o].reshape(rows, 2, HD) for o in range(ring)], 2)
    twice = jnp.concatenate([in_turn, in_turn], 2)
    ordered = lax.dynamic_slice_in_dim(twice, (ring - place) % ring, ring, 2)
    proj_grads = ordered.reshape(rows, 2, -1) / math.sqrt(token_count * group_count)

    new_first = ADAM_ONE * moment_first + (1 - ADAM_ONE) * proj_grads
    heads_kv = moment_second.shape[1]
    partial_squares = jnp.sum(
        jnp.square(proj_grads).reshape(rows, 2, heads_kv, -1), axis=(0, 3)
    )
    squares = taken_together(taken_together(partial_squares, DP), ("tensor",))
    new_second = ADAM_TWO * moment_second + (1 - ADAM_TWO) * squares / (D * HD)
    step_size = jnp.sqrt(new_second / (1 - ADAM_TWO**2)) + ADAM_EPS
    scaled = (new_first / (1 - ADAM_ONE**2)).reshape(rows, 2, heads_kv, -1)
    update = (scaled / step_size[None, :, :, None]).reshape(proj_grads.shape)
    return (update, new_first, new_second)


def solution(mesh):
    split = Mesh(
        mesh.devices.reshape(4, 4, 2, mesh.shape["tensor"]), ("dp_0", "dp_1", "dp_2", "tensor")
    )
    placed = (
        P(DP, "tensor"),
        P(DP, "tensor"),
        P(DP, None, "tensor"),
        P(DP, "tensor"),
        P(DP, "tensor"),
        P(DP, "tensor"),
        P(),
        P(),
        P(TENSOR_DP, None, None),
        P(),
    )
    return jax.shard_map(
        per_device,
        mesh=split,
        in_specs=placed,
        out_specs=(P(TENSOR_DP, None, None), P(TENSOR_DP, None, None), P()),
        check_vma=False,
    )
```

```python
import functools
import math

import jax
import jax.numpy as jnp
from jax import lax
from jax.experimental import pallas as pl
from jax.experimental.pallas import tpu as pltpu
from jax.sharding import Mesh
from jax.sharding import PartitionSpec as P

D = 4096
HD = 128
BLK = 128
DP = ("dp_0", "dp_1", "dp_2")
TENSOR_DP = ("tensor", "dp_0", "dp_1", "dp_2")

ADAM_ONE = 0.9
ADAM_TWO = 0.95
ADAM_EPS = 1e-08

NT = (((1,), (1,)), ((), ()))
NN = (((1,), (0,)), ((), ()))
TN = (((0,), (0,)), ((), ()))


def attention_kernel(
    first,
    per_step,
    tile_count,
    fill_ref,
    cont_ref,
    q_ref,
    q_next_ref,
    do_ref,
    do_next_ref,
    kv_ref,
    lse_ref,
    lse_next_ref,
    delta_ref,
    delta_next_ref,
    out_ref,
):
    heads = q_ref.shape[1] // HD
    scale_qk = HD ** (-0.5)
    base = first + pl.program_id(0) * per_step
    for j in range(per_step):
        tile = base + j
        rows = pl.ds(j * BLK, BLK)
        after = jnp.minimum(tile + 1, tile_count - 1)
        fill_own = fill_ref[tile]
        linked = jnp.where(tile + 1 < tile_count, cont_ref[after], 0)
        fill_next = jnp.where(linked == 1, fill_ref[after], 0)

        def window(ref, next_ref, h):
            columns = slice(h * HD, (h + 1) * HD)
            own = ref[rows, columns]
            if j + 1 < per_step:
                follow = ref[pl.ds((j + 1) * BLK, BLK), columns]
            else:
                follow = next_ref[:, columns]
            return [own, follow]

        def stat(ref, next_ref, h):
            own = ref[h : h + 1, pl.ds(j * BLK, BLK)]
            if j + 1 < per_step:
                follow = ref[h : h + 1, pl.ds((j + 1) * BLK, BLK)]
            else:
                follow = next_ref[h : h + 1, :]
            return [own.astype(jnp.float32), follow.astype(jnp.float32)]

        def stack(pick, ref, next_ref, axis):
            return jnp.concatenate(sum([pick(ref, next_ref, h) for h in range(heads)], []), axis)

        q_all = stack(window, q_ref, q_next_ref, 0)
        do_all = stack(window, do_ref, do_next_ref, 0)
        lse_row = stack(stat, lse_ref, lse_next_ref, 1)
        delta_row = stack(stat, delta_ref, delta_next_ref, 1)
        keys = kv_ref[0, rows, :]
        values = kv_ref[1, rows, :]
        scores = lax.dot_general(keys, q_all, NT, preferred_element_type=jnp.float32) * scale_qk
        dprobs = lax.dot_general(values, do_all, NT, preferred_element_type=jnp.float32)
        key_place = lax.broadcasted_iota(jnp.int32, (BLK, BLK), 0)
        query_place = lax.broadcasted_iota(jnp.int32, (BLK, BLK), 1)
        own_part = (query_place < fill_own) & (query_place >= key_place)
        next_part = query_place < fill_next
        allowed = jnp.concatenate([own_part, next_part] * heads, 1)
        probs = jnp.where(allowed, jnp.exp(scores - lse_row), 0.0)
        dscores = probs * (dprobs - delta_row)
        value_grad = lax.dot_general(
            probs.astype(jnp.bfloat16), do_all, NN, preferred_element_type=jnp.float32
        )
        key_grad = (
            lax.dot_general(
                dscores.astype(jnp.bfloat16), q_all, NN, preferred_element_type=jnp.float32
            )
            * scale_qk
        )
        out_ref[rows, 0:HD] = key_grad.astype(jnp.bfloat16)
        out_ref[rows, HD : 2 * HD] = value_grad.astype(jnp.bfloat16)


def attention(first, count, per_step, fill, cont, queries, out_grads, keys_values, lse, delta):
    tile_count = queries.shape[0] // BLK
    width = queries.shape[1]
    steps = count // per_step
    offset = first // per_step

    def own(i, *_):
        return (offset + i, 0)

    def follow(i, *_):
        return (jnp.minimum(first + (i + 1) * per_step, tile_count - 1), 0)

    def own_lanes(i, *_):
        return (0, offset + i)

    def follow_lanes(i, *_):
        return (0, jnp.minimum(first + (i + 1) * per_step, tile_count - 1))

    rows = per_step * BLK
    heads = lse.shape[0]
    return pl.pallas_call(
        functools.partial(attention_kernel, first, per_step, tile_count),
        grid_spec=pltpu.PrefetchScalarGridSpec(
            num_scalar_prefetch=2,
            grid=(steps,),
            in_specs=[
                pl.BlockSpec((rows, width), own),
                pl.BlockSpec((BLK, width), follow),
                pl.BlockSpec((rows, width), own),
                pl.BlockSpec((BLK, width), follow),
                pl.BlockSpec((2, rows, HD), lambda i, *_: (0, offset + i, 0)),
                pl.BlockSpec((heads, rows), own_lanes),
                pl.BlockSpec((heads, BLK), follow_lanes),
                pl.BlockSpec((heads, rows), own_lanes),
                pl.BlockSpec((heads, BLK), follow_lanes),
            ],
            out_specs=pl.BlockSpec((rows, 2 * HD), lambda i, *_: (i, 0)),
        ),
        out_shape=jax.ShapeDtypeStruct((count * BLK, 2 * HD), jnp.bfloat16),
        compiler_params=pltpu.CompilerParams(vmem_limit_bytes=32 * 1024 * 1024),
        cost_estimate=pl.CostEstimate(
            flops=count * 8 * heads * BLK * 2 * BLK * HD,
            bytes_accessed=count * BLK * 10 * HD * 2,
            transcendentals=count * heads * 2 * BLK * BLK,
        ),
        name="attention_grads",
    )(fill, cont, queries, queries, out_grads, out_grads, keys_values, lse, lse, delta, delta)


def product_kernel(turned_ref, *refs):
    *halves, out_ref = refs
    half = halves[0].shape[0]
    width = halves[0].shape[1]
    rows = turned_ref.shape[0]
    chunk = 256
    for i in range(len(halves) // 2):
        for r in range(0, rows, chunk):
            total = lax.dot_general(
                turned_ref[r : r + chunk, 0:half],
                halves[2 * i][...],
                NN,
                preferred_element_type=jnp.float32,
            ) + lax.dot_general(
                turned_ref[r : r + chunk, half : 2 * half],
                halves[2 * i + 1][...],
                NN,
                preferred_element_type=jnp.float32,
            )
            out_ref[r : r + chunk, i * width : (i + 1) * width] = total.astype(jnp.bfloat16)


def product(turned, pairs):
    halves = sum([list(pair) for pair in pairs], [])
    vmem = pl.BlockSpec(memory_space=pltpu.VMEM)
    return pl.pallas_call(
        product_kernel,
        in_specs=[vmem] * (1 + len(halves)),
        out_specs=vmem,
        out_shape=jax.ShapeDtypeStruct(
            (turned.shape[0], len(pairs) * halves[0].shape[1]), jnp.bfloat16
        ),
        compiler_params=pltpu.CompilerParams(vmem_limit_bytes=32 * 1024 * 1024),
        cost_estimate=pl.CostEstimate(flops=1000, bytes_accessed=1000, transcendentals=0),
        name="projection_product",
    )(turned, *halves)


def shifted(array, steps, length):
    return lax.ppermute(array, "tensor", [(i, (i + steps) % length) for i in range(length)])


def sum_at_owner(block, axes):
    length = lax.axis_size(axes)
    parts = block.reshape(length, -1, block.shape[1])
    arrived = lax.all_to_all(parts, axes, split_axis=0, concat_axis=0, tiled=True)
    return arrived.astype(jnp.float32).sum(axis=0)


def taken_together(array, axes):
    length = lax.axis_size(axes)
    everything = lax.all_to_all(
        jnp.broadcast_to(array[None], (length, *array.shape)), axes, 0, 0, tiled=True
    )
    return jnp.sum(everything, axis=0)


def per_device(
    layer_input,
    queries,
    keys_values,
    out_grads,
    log_sums,
    deltas,
    tile_fill,
    tile_cont,
    moment_first,
    moment_second,
):
    group_count = lax.axis_size(DP)
    ring = lax.axis_size("tensor")
    tile_count = tile_fill.shape[1]
    token_count = queries.shape[0]
    my_group = lax.axis_index(DP)
    place = lax.axis_index("tensor")
    fill = lax.dynamic_index_in_dim(tile_fill, my_group, 0, keepdims=False)
    cont = lax.dynamic_index_in_dim(tile_cont, my_group, 0, keepdims=False)
    kv = jnp.swapaxes(keys_values, 0, 1)
    half = tile_count // 2
    halves = [
        attention(first, half, 4, fill, cont, queries, out_grads, kv, log_sums.T, deltas.T)
        for first in (0, half)
    ]
    turned = layer_input.T

    blocks = {0: list(halves)}
    right, left = list(halves), list(halves)
    far = ring // 2
    for step in range(1, far):
        for part in range(2):
            right[part] = shifted(right[part], 1, ring)
            left[part] = shifted(left[part], -1, ring)
        blocks[-step] = list(right)
        blocks[step] = list(left)
    blocks[far] = [shifted(right[0], 1, ring), shifted(left[1], -1, ring)]

    summed = {}
    for offsets in ((0, -1, 1), (-2, 2), (-3, 3, far)):
        total = sum_at_owner(product(turned, [blocks[o] for o in offsets]), DP)
        for i, o in enumerate(offsets):
            summed[o % ring] = total[:, i * 2 * HD : (i + 1) * 2 * HD]

    rows = moment_first.shape[0]
    in_turn = jnp.stack([summed[o].reshape(rows, 2, HD) for o in range(ring)], 2)
    twice = jnp.concatenate([in_turn, in_turn], 2)
    ordered = lax.dynamic_slice_in_dim(twice, (ring - place) % ring, ring, 2)
    proj_grads = ordered.reshape(rows, 2, -1) / math.sqrt(token_count * group_count)

    new_first = ADAM_ONE * moment_first + (1 - ADAM_ONE) * proj_grads
    heads_kv = moment_second.shape[1]
    partial_squares = jnp.sum(
        jnp.square(proj_grads).reshape(rows, 2, heads_kv, -1), axis=(0, 3)
    )
    squares = taken_together(taken_together(partial_squares, DP), ("tensor",))
    new_second = ADAM_TWO * moment_second + (1 - ADAM_TWO) * squares / (D * HD)
    step_size = jnp.sqrt(new_second / (1 - ADAM_TWO**2)) + ADAM_EPS
    scaled = (new_first / (1 - ADAM_ONE**2)).reshape(rows, 2, heads_kv, -1)
    update = (scaled / step_size[None, :, :, None]).reshape(proj_grads.shape)
    return (update, new_first, new_second)


def solution(mesh):
    split = Mesh(
        mesh.devices.reshape(4, 4, 2, mesh.shape["tensor"]), ("dp_0", "dp_1", "dp_2", "tensor")
    )
    placed = (
        P(DP, "tensor"),
        P(DP, "tensor"),
        P(DP, None, "tensor"),
        P(DP, "tensor"),
        P(DP, "tensor"),
        P(DP, "tensor"),
        P(),
        P(),
        P(TENSOR_DP, None, None),
        P(),
    )
    return jax.shard_map(
        per_device,
        mesh=split,
        in_specs=placed,
        out_specs=(P(TENSOR_DP, None, None), P(TENSOR_DP, None, None), P()),
        check_vma=False,
    )
```

```python
import functools
import math

import jax
import jax.numpy as jnp
from jax import lax
from jax.experimental import pallas as pl
from jax.experimental.pallas import tpu as pltpu
from jax.sharding import Mesh
from jax.sharding import PartitionSpec as P

D = 4096
HD = 128
BLK = 128
DP = ("dp_0", "dp_1", "dp_2")
TENSOR_DP = ("tensor", "dp_0", "dp_1", "dp_2")

ADAM_ONE = 0.9
ADAM_TWO = 0.95
ADAM_EPS = 1e-08

NT = (((1,), (1,)), ((), ()))
NN = (((1,), (0,)), ((), ()))
TN = (((0,), (0,)), ((), ()))


def attention_kernel(
    first,
    per_step,
    tile_count,
    fill_ref,
    cont_ref,
    q_ref,
    q_next_ref,
    do_ref,
    do_next_ref,
    kv_ref,
    lse_ref,
    lse_next_ref,
    delta_ref,
    delta_next_ref,
    out_ref,
):
    heads = q_ref.shape[1] // HD
    scale_qk = HD ** (-0.5)
    base = first + pl.program_id(0) * per_step
    for j in range(per_step):
        tile = base + j
        rows = pl.ds(j * BLK, BLK)
        after = jnp.minimum(tile + 1, tile_count - 1)
        fill_own = fill_ref[tile]
        linked = jnp.where(tile + 1 < tile_count, cont_ref[after], 0)
        fill_next = jnp.where(linked == 1, fill_ref[after], 0)

        def window(ref, next_ref, h):
            columns = slice(h * HD, (h + 1) * HD)
            own = ref[rows, columns]
            if j + 1 < per_step:
                follow = ref[pl.ds((j + 1) * BLK, BLK), columns]
            else:
                follow = next_ref[:, columns]
            return [own, follow]

        def stat(ref, next_ref, h):
            own = ref[h : h + 1, pl.ds(j * BLK, BLK)]
            if j + 1 < per_step:
                follow = ref[h : h + 1, pl.ds((j + 1) * BLK, BLK)]
            else:
                follow = next_ref[h : h + 1, :]
            return [own.astype(jnp.float32), follow.astype(jnp.float32)]

        def stack(pick, ref, next_ref, axis):
            return jnp.concatenate(sum([pick(ref, next_ref, h) for h in range(heads)], []), axis)

        q_all = stack(window, q_ref, q_next_ref, 0)
        do_all = stack(window, do_ref, do_next_ref, 0)
        lse_row = stack(stat, lse_ref, lse_next_ref, 1)
        delta_row = stack(stat, delta_ref, delta_next_ref, 1)
        keys = kv_ref[0, rows, :]
        values = kv_ref[1, rows, :]
        scores = lax.dot_general(keys, q_all, NT, preferred_element_type=jnp.float32) * scale_qk
        dprobs = lax.dot_general(values, do_all, NT, preferred_element_type=jnp.float32)
        key_place = lax.broadcasted_iota(jnp.int32, (BLK, BLK), 0)
        query_place = lax.broadcasted_iota(jnp.int32, (BLK, BLK), 1)
        own_part = (query_place < fill_own) & (query_place >= key_place)
        next_part = query_place < fill_next
        allowed = jnp.concatenate([own_part, next_part] * heads, 1)
        probs = jnp.where(allowed, jnp.exp(scores - lse_row), 0.0)
        dscores = probs * (dprobs - delta_row)
        value_grad = lax.dot_general(
            probs.astype(jnp.bfloat16), do_all, NN, preferred_element_type=jnp.float32
        )
        key_grad = (
            lax.dot_general(
                dscores.astype(jnp.bfloat16), q_all, NN, preferred_element_type=jnp.float32
            )
            * scale_qk
        )
        out_ref[rows, 0:HD] = key_grad.astype(jnp.bfloat16)
        out_ref[rows, HD : 2 * HD] = value_grad.astype(jnp.bfloat16)


def attention(first, count, per_step, fill, cont, queries, out_grads, keys_values, lse, delta):
    tile_count = queries.shape[0] // BLK
    width = queries.shape[1]
    steps = count // per_step
    offset = first // per_step

    def own(i, *_):
        return (offset + i, 0)

    def follow(i, *_):
        return (jnp.minimum(first + (i + 1) * per_step, tile_count - 1), 0)

    def own_lanes(i, *_):
        return (0, offset + i)

    def follow_lanes(i, *_):
        return (0, jnp.minimum(first + (i + 1) * per_step, tile_count - 1))

    rows = per_step * BLK
    heads = lse.shape[0]
    return pl.pallas_call(
        functools.partial(attention_kernel, first, per_step, tile_count),
        grid_spec=pltpu.PrefetchScalarGridSpec(
            num_scalar_prefetch=2,
            grid=(steps,),
            in_specs=[
                pl.BlockSpec((rows, width), own),
                pl.BlockSpec((BLK, width), follow),
                pl.BlockSpec((rows, width), own),
                pl.BlockSpec((BLK, width), follow),
                pl.BlockSpec((2, rows, HD), lambda i, *_: (0, offset + i, 0)),
                pl.BlockSpec((heads, rows), own_lanes),
                pl.BlockSpec((heads, BLK), follow_lanes),
                pl.BlockSpec((heads, rows), own_lanes),
                pl.BlockSpec((heads, BLK), follow_lanes),
            ],
            out_specs=pl.BlockSpec((rows, 2 * HD), lambda i, *_: (i, 0)),
        ),
        out_shape=jax.ShapeDtypeStruct((count * BLK, 2 * HD), jnp.bfloat16),
        compiler_params=pltpu.CompilerParams(vmem_limit_bytes=32 * 1024 * 1024),
        cost_estimate=pl.CostEstimate(
            flops=count * 8 * heads * BLK * 2 * BLK * HD,
            bytes_accessed=count * BLK * 10 * HD * 2,
            transcendentals=count * heads * 2 * BLK * BLK,
        ),
        name="attention_grads",
    )(fill, cont, queries, queries, out_grads, out_grads, keys_values, lse, lse, delta, delta)


def product_kernel(offset, turned_ref, *refs):
    halves, out_ref = refs[: len(refs) // 2 * 2], refs[-1]
    if len(refs) % 2 == 0:
        halves = refs[:-2]
    half = halves[0].shape[0]
    width = halves[0].shape[1]
    rows = turned_ref.shape[0]
    chunk = 256
    for i in range(len(halves) // 2):
        for r in range(0, rows, chunk):
            total = lax.dot_general(
                turned_ref[r : r + chunk, 0:half],
                halves[2 * i][...],
                NN,
                preferred_element_type=jnp.float32,
            ) + lax.dot_general(
                turned_ref[r : r + chunk, half : 2 * half],
                halves[2 * i + 1][...],
                NN,
                preferred_element_type=jnp.float32,
            )
            first = offset + i * width
            out_ref[r : r + chunk, first : first + width] = total.astype(jnp.bfloat16)


def product(turned, pairs, offset=0, total=None, filled=None):
    halves = sum([list(pair) for pair in pairs], [])
    total = total or len(pairs)
    operands = [turned, *halves] + ([] if filled is None else [filled])
    vmem = pl.BlockSpec(memory_space=pltpu.VMEM)
    width = halves[0].shape[1]
    return pl.pallas_call(
        functools.partial(product_kernel, offset * width),
        in_specs=[vmem] * len(operands),
        out_specs=vmem,
        out_shape=jax.ShapeDtypeStruct((turned.shape[0], total * width), jnp.bfloat16),
        input_output_aliases={} if filled is None else {len(operands) - 1: 0},
        compiler_params=pltpu.CompilerParams(vmem_limit_bytes=12 * 1024 * 1024),
        cost_estimate=pl.CostEstimate(flops=int(1300000000.0*len(pairs)), bytes_accessed=1000, transcendentals=0),
        name="projection_product",
    )(*operands)


def shifted(array, steps, length):
    return lax.ppermute(array, "tensor", [(i, (i + steps) % length) for i in range(length)])


def sum_at_owner(block, axes):
    length = lax.axis_size(axes)
    parts = block.reshape(length, -1, block.shape[1])
    arrived = lax.all_to_all(parts, axes, split_axis=0, concat_axis=0, tiled=True)
    return arrived.astype(jnp.float32).sum(axis=0)


def taken_together(array, axes):
    length = lax.axis_size(axes)
    everything = lax.all_to_all(
        jnp.broadcast_to(array[None], (length, *array.shape)), axes, 0, 0, tiled=True
    )
    return jnp.sum(everything, axis=0)


def per_device(
    layer_input,
    queries,
    keys_values,
    out_grads,
    log_sums,
    deltas,
    tile_fill,
    tile_cont,
    moment_first,
    moment_second,
):
    group_count = lax.axis_size(DP)
    ring = lax.axis_size("tensor")
    tile_count = tile_fill.shape[1]
    token_count = queries.shape[0]
    my_group = lax.axis_index(DP)
    place = lax.axis_index("tensor")
    fill = lax.dynamic_index_in_dim(tile_fill, my_group, 0, keepdims=False)
    cont = lax.dynamic_index_in_dim(tile_cont, my_group, 0, keepdims=False)
    kv = jnp.swapaxes(keys_values, 0, 1)
    half = tile_count // 2
    halves = [
        attention(first, half, 4, fill, cont, queries, out_grads, kv, log_sums.T, deltas.T)
        for first in (0, half)
    ]
    turned = layer_input.T

    blocks = {0: list(halves)}
    right, left = list(halves), list(halves)
    far = ring // 2
    for step in range(1, 4):
        for part in range(2):
            right[part] = shifted(right[part], 1, ring)
            left[part] = shifted(left[part], -1, ring)
        blocks[-step] = list(right)
        blocks[step] = list(left)
    blocks[far] = [shifted(right[0], 1, ring), shifted(left[1], -1, ring)]

    summed = {}

    def keep(offsets, together):
        total = sum_at_owner(together, DP)
        for i, o in enumerate(offsets):
            summed[o % ring] = total[:, i * 2 * HD : (i + 1) * 2 * HD]

    for group in ((0, -1, 1), (-2, 2), (-3, 3, 4)):
        keep(group, product(turned, [blocks[o] for o in group]))

    rows = moment_first.shape[0]
    in_turn = jnp.stack([summed[o].reshape(rows, 2, HD) for o in range(ring)], 2)
    twice = jnp.concatenate([in_turn, in_turn], 2)
    ordered = lax.dynamic_slice_in_dim(twice, (ring - place) % ring, ring, 2)
    proj_grads = ordered.reshape(rows, 2, -1) / math.sqrt(token_count * group_count)

    new_first = ADAM_ONE * moment_first + (1 - ADAM_ONE) * proj_grads
    heads_kv = moment_second.shape[1]
    partial_squares = jnp.sum(
        jnp.square(proj_grads).reshape(rows, 2, heads_kv, -1), axis=(0, 3)
    )
    squares = taken_together(taken_together(partial_squares, ("dp_2", "tensor")), ("dp_0", "dp_1"))
    new_second = ADAM_TWO * moment_second + (1 - ADAM_TWO) * squares / (D * HD)
    step_size = jnp.sqrt(new_second / (1 - ADAM_TWO**2)) + ADAM_EPS
    scaled = (new_first / (1 - ADAM_ONE**2)).reshape(rows, 2, heads_kv, -1)
    update = (scaled / step_size[None, :, :, None]).reshape(proj_grads.shape)
    return (update, new_first, new_second)


def solution(mesh):
    split = Mesh(
        mesh.devices.reshape(4, 4, 2, mesh.shape["tensor"]), ("dp_0", "dp_1", "dp_2", "tensor")
    )
    placed = (
        P(DP, "tensor"),
        P(DP, "tensor"),
        P(DP, None, "tensor"),
        P(DP, "tensor"),
        P(DP, "tensor"),
        P(DP, "tensor"),
        P(),
        P(),
        P(TENSOR_DP, None, None),
        P(),
    )
    return jax.shard_map(
        per_device,
        mesh=split,
        in_specs=placed,
        out_specs=(P(TENSOR_DP, None, None), P(TENSOR_DP, None, None), P()),
        check_vma=False,
    )
```

```python
import functools
import math

import jax
import jax.numpy as jnp
from jax import lax
from jax.experimental import pallas as pl
from jax.experimental.pallas import tpu as pltpu
from jax.sharding import Mesh
from jax.sharding import PartitionSpec as P

D = 4096
HD = 128
BLK = 128
DP = ("dp_0", "dp_1", "dp_2")
TENSOR_DP = ("tensor", "dp_0", "dp_1", "dp_2")

ADAM_ONE = 0.9
ADAM_TWO = 0.95
ADAM_EPS = 1e-08

NT = (((1,), (1,)), ((), ()))
NN = (((1,), (0,)), ((), ()))
TN = (((0,), (0,)), ((), ()))


def attention_kernel(
    first,
    per_step,
    tile_count,
    fill_ref,
    cont_ref,
    q_ref,
    q_next_ref,
    do_ref,
    do_next_ref,
    kv_ref,
    lse_ref,
    lse_next_ref,
    delta_ref,
    delta_next_ref,
    out_ref,
):
    heads = q_ref.shape[1] // HD
    scale_qk = HD ** (-0.5)
    base = first + pl.program_id(0) * per_step
    for j in range(per_step):
        tile = base + j
        rows = pl.ds(j * BLK, BLK)
        after = jnp.minimum(tile + 1, tile_count - 1)
        fill_own = fill_ref[tile]
        linked = jnp.where(tile + 1 < tile_count, cont_ref[after], 0)
        fill_next = jnp.where(linked == 1, fill_ref[after], 0)

        def window(ref, next_ref, h):
            columns = slice(h * HD, (h + 1) * HD)
            own = ref[rows, columns]
            if j + 1 < per_step:
                follow = ref[pl.ds((j + 1) * BLK, BLK), columns]
            else:
                follow = next_ref[:, columns]
            return [own, follow]

        def stat(ref, next_ref, h):
            own = ref[h : h + 1, pl.ds(j * BLK, BLK)]
            if j + 1 < per_step:
                follow = ref[h : h + 1, pl.ds((j + 1) * BLK, BLK)]
            else:
                follow = next_ref[h : h + 1, :]
            return [own.astype(jnp.float32), follow.astype(jnp.float32)]

        def stack(pick, ref, next_ref, axis):
            return jnp.concatenate(sum([pick(ref, next_ref, h) for h in range(heads)], []), axis)

        q_all = stack(window, q_ref, q_next_ref, 0)
        do_all = stack(window, do_ref, do_next_ref, 0)
        lse_row = stack(stat, lse_ref, lse_next_ref, 1)
        delta_row = stack(stat, delta_ref, delta_next_ref, 1)
        keys = kv_ref[0, rows, :]
        values = kv_ref[1, rows, :]
        scores = lax.dot_general(keys, q_all, NT, preferred_element_type=jnp.float32) * scale_qk
        dprobs = lax.dot_general(values, do_all, NT, preferred_element_type=jnp.float32)
        key_place = lax.broadcasted_iota(jnp.int32, (BLK, BLK), 0)
        query_place = lax.broadcasted_iota(jnp.int32, (BLK, BLK), 1)
        own_part = (query_place < fill_own) & (query_place >= key_place)
        next_part = query_place < fill_next
        allowed = jnp.concatenate([own_part, next_part] * heads, 1)
        probs = jnp.where(allowed, jnp.exp(scores - lse_row), 0.0)
        dscores = probs * (dprobs - delta_row)
        value_grad = lax.dot_general(
            probs.astype(jnp.bfloat16), do_all, NN, preferred_element_type=jnp.float32
        )
        key_grad = (
            lax.dot_general(
                dscores.astype(jnp.bfloat16), q_all, NN, preferred_element_type=jnp.float32
            )
            * scale_qk
        )
        out_ref[rows, 0:HD] = key_grad.astype(jnp.bfloat16)
        out_ref[rows, HD : 2 * HD] = value_grad.astype(jnp.bfloat16)


def attention(first, count, per_step, fill, cont, queries, out_grads, keys_values, lse, delta):
    tile_count = queries.shape[0] // BLK
    width = queries.shape[1]
    steps = count // per_step
    offset = first // per_step

    def own(i, *_):
        return (offset + i, 0)

    def follow(i, *_):
        return (jnp.minimum(first + (i + 1) * per_step, tile_count - 1), 0)

    def own_lanes(i, *_):
        return (0, offset + i)

    def follow_lanes(i, *_):
        return (0, jnp.minimum(first + (i + 1) * per_step, tile_count - 1))

    rows = per_step * BLK
    heads = lse.shape[0]
    return pl.pallas_call(
        functools.partial(attention_kernel, first, per_step, tile_count),
        grid_spec=pltpu.PrefetchScalarGridSpec(
            num_scalar_prefetch=2,
            grid=(steps,),
            in_specs=[
                pl.BlockSpec((rows, width), own),
                pl.BlockSpec((BLK, width), follow),
                pl.BlockSpec((rows, width), own),
                pl.BlockSpec((BLK, width), follow),
                pl.BlockSpec((2, rows, HD), lambda i, *_: (0, i, 0)),
                pl.BlockSpec((heads, rows), own_lanes),
                pl.BlockSpec((heads, BLK), follow_lanes),
                pl.BlockSpec((heads, rows), own_lanes),
                pl.BlockSpec((heads, BLK), follow_lanes),
            ],
            out_specs=pl.BlockSpec((rows, 2 * HD), lambda i, *_: (i, 0)),
        ),
        out_shape=jax.ShapeDtypeStruct((count * BLK, 2 * HD), jnp.bfloat16),
        compiler_params=pltpu.CompilerParams(vmem_limit_bytes=32 * 1024 * 1024),
        cost_estimate=pl.CostEstimate(
            flops=count * 8 * heads * BLK * 2 * BLK * HD,
            bytes_accessed=count * BLK * 10 * HD * 2,
            transcendentals=count * heads * 2 * BLK * BLK,
        ),
        name="attention_grads",
    )(fill, cont, queries, queries, out_grads, out_grads, keys_values, lse, lse, delta, delta)


def product_kernel(offset, turned_ref, *refs):
    halves, out_ref = refs[: len(refs) // 2 * 2], refs[-1]
    if len(refs) % 2 == 0:
        halves = refs[:-2]
    half = halves[0].shape[0]
    width = halves[0].shape[1]
    rows = turned_ref.shape[0]
    chunk = rows
    for i in range(len(halves) // 2):
        for r in range(0, rows, chunk):
            total = lax.dot_general(
                turned_ref[r : r + chunk, 0:half],
                halves[2 * i][...],
                NN,
                preferred_element_type=jnp.float32,
            ) + lax.dot_general(
                turned_ref[r : r + chunk, half : 2 * half],
                halves[2 * i + 1][...],
                NN,
                preferred_element_type=jnp.float32,
            )
            first = offset + i * width
            out_ref[r : r + chunk, first : first + width] = total.astype(jnp.bfloat16)


def product(turned, pairs, offset=0, total=None, filled=None):
    halves = sum([list(pair) for pair in pairs], [])
    total = total or len(pairs)
    operands = [turned, *halves] + ([] if filled is None else [filled])
    vmem = pl.BlockSpec(memory_space=pltpu.VMEM)
    width = halves[0].shape[1]
    return pl.pallas_call(
        functools.partial(product_kernel, offset * width),
        in_specs=[vmem] * len(operands),
        out_specs=vmem,
        out_shape=jax.ShapeDtypeStruct((turned.shape[0], total * width), jnp.bfloat16),
        input_output_aliases={} if filled is None else {len(operands) - 1: 0},
        compiler_params=pltpu.CompilerParams(vmem_limit_bytes=12 * 1024 * 1024),
        cost_estimate=pl.CostEstimate(flops=1300000000 * len(pairs), bytes_accessed=1000, transcendentals=0),
        name="projection_product",
    )(*operands)


def shifted(array, steps, length):
    return lax.ppermute(array, "tensor", [(i, (i + steps) % length) for i in range(length)])


def sum_at_owner(block, axes):
    length = lax.axis_size(axes)
    parts = block.reshape(length, -1, block.shape[1])
    arrived = lax.all_to_all(parts, axes, split_axis=0, concat_axis=0, tiled=True)
    return arrived.astype(jnp.float32).sum(axis=0)


def taken_together(array, axes):
    length = lax.axis_size(axes)
    everything = lax.all_to_all(
        jnp.broadcast_to(array[None], (length, *array.shape)), axes, 0, 0, tiled=True
    )
    return jnp.sum(everything, axis=0)


def per_device(
    layer_input,
    queries,
    keys_values,
    out_grads,
    log_sums,
    deltas,
    tile_fill,
    tile_cont,
    moment_first,
    moment_second,
):
    group_count = lax.axis_size(DP)
    ring = lax.axis_size("tensor")
    tile_count = tile_fill.shape[1]
    token_count = queries.shape[0]
    my_group = lax.axis_index(DP)
    place = lax.axis_index("tensor")
    fill = lax.dynamic_index_in_dim(tile_fill, my_group, 0, keepdims=False)
    cont = lax.dynamic_index_in_dim(tile_cont, my_group, 0, keepdims=False)
    half = tile_count // 2
    halves = [
        attention(first, half, 8, fill, cont, queries, out_grads, jnp.swapaxes(keys_values[first * BLK : (first + half) * BLK], 0, 1), log_sums.T, deltas.T)
        for first in (0, half)
    ]
    turned = layer_input.T

    blocks = {0: list(halves)}
    right, left = list(halves), list(halves)
    far = ring // 2
    for step in range(1, 4):
        for part in range(2):
            right[part] = shifted(right[part], 1, ring)
            left[part] = shifted(left[part], -1, ring)
        blocks[-step] = list(right)
        blocks[step] = list(left)
    blocks[far] = [shifted(right[0], 1, ring), shifted(left[1], -1, ring)]

    summed = {}

    def keep(offsets, together):
        total = sum_at_owner(together, DP)
        for i, o in enumerate(offsets):
            summed[o % ring] = total[:, i * 2 * HD : (i + 1) * 2 * HD]

    for group in ((0, -1, 1), (-2, 2), (-3, 3, 4)):
        keep(group, product(turned, [blocks[o] for o in group]))

    rows = moment_first.shape[0]
    in_turn = jnp.stack([summed[o].reshape(rows, 2, HD) for o in range(ring)], 2)
    twice = jnp.concatenate([in_turn, in_turn], 2)
    ordered = lax.dynamic_slice_in_dim(twice, (ring - place) % ring, ring, 2)
    proj_grads = ordered.reshape(rows, 2, -1) / math.sqrt(token_count * group_count)

    new_first = ADAM_ONE * moment_first + (1 - ADAM_ONE) * proj_grads
    heads_kv = moment_second.shape[1]
    partial_squares = jnp.sum(
        jnp.square(proj_grads).reshape(rows, 2, heads_kv, -1), axis=(0, 3)
    )
    squares = taken_together(taken_together(partial_squares, ("dp_2", "tensor")), ("dp_0", "dp_1"))
    new_second = ADAM_TWO * moment_second + (1 - ADAM_TWO) * squares / (D * HD)
    step_size = jnp.sqrt(new_second / (1 - ADAM_TWO**2)) + ADAM_EPS
    scaled = (new_first / (1 - ADAM_ONE**2)).reshape(rows, 2, heads_kv, -1)
    update = (scaled / step_size[None, :, :, None]).reshape(proj_grads.shape)
    return (update, new_first, new_second)


def solution(mesh):
    split = Mesh(
        mesh.devices.reshape(4, 4, 2, mesh.shape["tensor"]), ("dp_0", "dp_1", "dp_2", "tensor")
    )
    placed = (
        P(DP, "tensor"),
        P(DP, "tensor"),
        P(DP, None, "tensor"),
        P(DP, "tensor"),
        P(DP, "tensor"),
        P(DP, "tensor"),
        P(),
        P(),
        P(TENSOR_DP, None, None),
        P(),
    )
    return jax.shard_map(
        per_device,
        mesh=split,
        in_specs=placed,
        out_specs=(P(TENSOR_DP, None, None), P(TENSOR_DP, None, None), P()),
        check_vma=False,
    )
```
